32 devices in a mesh: blk: 16 (over z, y, core), grp: 2 (over x).
Axes of the slice: x: 2, y: 2, z: 4, core: 2. Of those that a mesh axis runs over, the one named last changes fastest.
Arguments:
- left_env: bfloat16 [16, 24, 256, 256], P('blk', 'grp'), may hold values from -0.375 to 0.375
- right_env: bfloat16 [32, 24, 256, 256], P(('blk', 'grp')), may hold values from -0.078125 to 0.078125
- psi: bfloat16 [32, 1, 256, 256], P(('blk', 'grp')), may hold values from -6 to 6
- pairing: int32 [32, 1], P(('blk', 'grp')), may hold values from 0 to 15, as said below
- left_size: int32 [16], replicated, may hold values from 64 to 256, as said below
- right_size: int32 [32], P(('blk', 'grp')), may hold values from 64 to 256, as said below
Outputs:
- result: bfloat16 [32, 1, 256, 256], P(('blk', 'grp'))
The draws below stay inside these ranges and needn't reach their ends.
Inputs may be any that keep to these rules, and one draw needn't show every extreme that they name: `pairing`: the 1 left sectors of one right sector are distinct. `left_size`: some left sector has exactly 256 live rows. `right_size`: some right sector has exactly 256 live columns.
All inputs are finite; a program needn't handle non-finite values.
Results may differ from the reference program's by a relative error of at most 0.005.
Values may be sent and summed in bfloat16 or wider, within the bound.
A program may use at most 64 MiB of HBM per device.

```python
import jax
import jax.numpy as jnp
from jax import lax

SEC = 256
A = 24
PER_R = 1
NL = 16
NR = 32


def sized_draw(key, length):
    first_key, second_key = jax.random.split(key)
    drawn = jax.random.randint(first_key, (length,), SEC // 4, SEC + 1)
    fullest = jax.random.randint(second_key, (), 0, length)
    return jnp.where(jnp.arange(length) == fullest, SEC, drawn).astype(jnp.int32)


def draw_left_size(key, part):
    return sized_draw(jax.random.fold_in(key, 11), NL)


def draw_right_size(key, part):
    return sized_draw(jax.random.fold_in(key, 12), NR)


def draw_pairing(key, part):
    first_key, second_key, third_key, fourth_key = jax.random.split(jax.random.fold_in(key, 13), 4)
    favour = jax.random.randint(first_key, (NL,), 0, 4) * (NL * 4)
    scores = jax.random.randint(second_key, (NR, NL), 0, NL * 4) + favour[None, :]
    scores = scores * NL + jnp.arange(NL)[None, :]
    picked_scores, picked = lax.top_k(scores, PER_R)
    picked = picked.astype(jnp.int32)
    low_row = jax.random.randint(third_key, (), 0, NR).astype(jnp.int32)
    step_row = jax.random.randint(fourth_key, (), 1, NR).astype(jnp.int32)
    high_row = (low_row + step_row) % NR
    slots = jnp.arange(PER_R).astype(jnp.int32)
    rows = jnp.arange(NR).astype(jnp.int32)[:, None]
    picked = jnp.where(rows == low_row, slots[None, :], picked)
    picked = jnp.where(rows == high_row, (NL - 1 - slots)[None, :], picked)
    return picked.astype(jnp.int32)


def steps_of(rng, shape, cuts, least, high):
    loudness, own = 1.0, jax.random.fold_in(rng, 6)
    for axis_at, shards_of in cuts:
        steps = jnp.exp(jax.random.uniform(jax.random.fold_in(own, axis_at), (shards_of,), jnp.float32, least / len(cuts), high / len(cuts)))
        loudness = loudness * jnp.repeat(steps, shape[axis_at] // shards_of).reshape([-1 if axis == axis_at else 1 for axis in range(len(shape))])
    return loudness


def bell_draw(rng, dims, deviation, bound, pieces=(), held_as=jnp.bfloat16):
    values = deviation * jax.random.normal(rng, dims, jnp.float32)
    if pieces:
        values = values * steps_of(rng, dims, pieces, -0.22, 0.18)
    return jnp.clip(values, -bound, bound).astype(held_as)


def setup_inputs(seed: int = 0) -> dict:
    arg_keys = jax.random.split(jax.random.key(seed), 7)
    return {
        "left_env": bell_draw(arg_keys[0], (NL, A, SEC, SEC), SEC ** -0.5, 0.375, ((0, 16), (1, 2))),
        "right_env": bell_draw(arg_keys[1], (NR, A, SEC, SEC), (A * SEC) ** -0.5, 0.078125, ((0, 32),)),
        "psi": bell_draw(arg_keys[2], (NR, PER_R, SEC, SEC), 1.0, 6.0, ((0, 32),)),
        "pairing": draw_pairing(jax.random.fold_in(arg_keys[6], 71), 0),
        "left_size": draw_left_size(jax.random.fold_in(arg_keys[6], 71), 0),
        "right_size": draw_right_size(jax.random.fold_in(arg_keys[6], 71), 0),
    }


def reference(left_env, right_env, psi, pairing, left_size, right_size):
    cells = jnp.arange(SEC)

    def per_sector(inputs):
        right_block, tiles_here, lefts_here, right_rows = inputs
        column_mask = cells < right_rows
        right_flat = right_block.reshape(A * SEC, SEC)

        def per_pair(pair_inputs):
            psi_tile, left_index = pair_inputs
            left_rows = left_size[left_index]
            live_mask = (cells[:, None] < left_rows) & column_mask[None, :]
            masked = jnp.where(live_mask, psi_tile, jnp.zeros((), jnp.bfloat16))
            left_block = left_env[left_index]
            contracted = jnp.einsum("alk,kr->lar", left_block.astype(jnp.float32), masked.astype(jnp.float32)).astype(jnp.bfloat16)
            product = jnp.dot(contracted.reshape(SEC, A * SEC), right_flat, preferred_element_type=jnp.float32)
            return jnp.where(live_mask, product, jnp.zeros((), jnp.float32)).astype(jnp.bfloat16)

        return lax.map(per_pair, (tiles_here, lefts_here))

    return lax.map(per_sector, (right_env, psi, pairing, right_size))
```

```python
import functools

import jax
import jax.numpy as jnp
from jax import lax
from jax.experimental import pallas as pl
from jax.experimental.pallas import tpu as pltpu
from jax.sharding import PartitionSpec as P

PLANE = 4
SLOTS = (4, 8)


def live_mask_of(shape, rows, cols):
    row = lax.broadcasted_iota(jnp.int32, shape, 0)
    col = lax.broadcasted_iota(jnp.int32, shape, 1)
    return (row < rows) & (col < cols)


def spread_kernel(
    ranks, groups, pairing, left_size, right_size, psi, table_out, psis_out,
    mine, table, send, recv, tsend, trecv,
):
    members = PLANE * groups
    me = lax.axis_index("blk") * groups + lax.axis_index("grp")
    base, slot = me // members * members, lax.rem(me, members)

    def at(rank):
        return {"blk": rank // groups, "grp": lax.rem(rank, groups)}

    barrier = pltpu.get_barrier_semaphore()

    @pl.loop(1, ranks)
    def _(k):
        pl.semaphore_signal(barrier, inc=1, device_id=at(lax.rem(me + k, ranks)))

    left = pairing[0, 0]
    live = live_mask_of(psi.shape[2:], left_size[left], right_size[0])
    psis_out[slot] = jnp.where(live, psi[0, 0].astype(jnp.float32), 0.0).astype(jnp.bfloat16)
    mine[...] = jnp.full(mine.shape, left, jnp.int32)
    table[me] = jnp.full(mine.shape, left, jnp.int32)
    pl.semaphore_wait(barrier, ranks - 1)

    def entry(k, to, where):
        return pltpu.make_async_remote_copy(
            src_ref=mine, dst_ref=table.at[where], send_sem=tsend.at[k], recv_sem=trecv.at[k],
            device_id=at(to))

    def tile(k, to, where):
        return pltpu.make_async_remote_copy(
            src_ref=psis_out.at[where], dst_ref=psis_out.at[where], send_sem=send.at[k],
            recv_sem=recv.at[k], device_id=at(to))

    @pl.loop(1, ranks)
    def _(k):
        entry(k, lax.rem(me + k, ranks), me).start()

    @pl.loop(1, members)
    def _(k):
        tile(k, base + lax.rem(slot + k, members), slot).start()

    @pl.loop(1, ranks)
    def _(k):
        back = lax.rem(me + ranks - k, ranks)
        entry(k, back, back).wait_recv()
        entry(k, lax.rem(me + k, ranks), me).wait_send()

    @pl.loop(1, members)
    def _(k):
        back = lax.rem(slot + members - k, members)
        tile(k, base + back, back).wait_recv()
        tile(k, base + lax.rem(slot + k, members), slot).wait_send()

    table_out[...] = table[...]


def apply_kernel(
    count, planes, groups, up_src, down_src, tile_at, own_size, psis, left_env, right_env, out,
    pool, staged, rights, parts, arrived,
    lsend, lrecv, rsend, rrecv, zsend, zrecv, psend, precv, local,
):
    members = PLANE * groups
    width = pool.shape[1]
    blk, grp = lax.axis_index("blk"), lax.axis_index("grp")
    z, q = blk // PLANE, lax.rem(blk, PLANE)
    slot = q * groups + grp
    half = left_env.shape[1]
    has_below, has_above = z > 0, z < planes - 1

    def peer(index):
        return {"blk": z * PLANE + index // groups, "grp": lax.rem(index, groups)}

    barrier = pltpu.get_barrier_semaphore()

    @pl.loop(1, members)
    def _(k):
        pl.semaphore_signal(barrier, inc=1, device_id=peer(lax.rem(slot + k, members)))

    @pl.when(has_below)
    def _():
        pl.semaphore_signal(barrier, inc=1, device_id={"blk": blk - PLANE, "grp": grp})

    @pl.when(has_above)
    def _():
        pl.semaphore_signal(barrier, inc=1, device_id={"blk": blk + PLANE, "grp": grp})

    left_own = pltpu.make_async_copy(left_env.at[0, pl.ds(q * width, width)], pool.at[q], local.at[0])
    right_own = pltpu.make_async_copy(
        right_env.at[0, pl.ds(grp * half + q * width, width)], rights.at[slot], local.at[1])
    left_own.start()
    right_own.start()
    pl.semaphore_wait(barrier, members - 1 + has_below.astype(jnp.int32) + has_above.astype(jnp.int32))

    def left_copy(k, to, where):
        return pltpu.make_async_remote_copy(
            src_ref=left_env.at[0, pl.ds(to * width, width)], dst_ref=pool.at[where],
            send_sem=lsend.at[k], recv_sem=lrecv.at[k],
            device_id={"blk": z * PLANE + to, "grp": grp})

    def right_copy(k, to, where):
        first = lax.rem(to, groups) * half + to // groups * width
        return pltpu.make_async_remote_copy(
            src_ref=right_env.at[0, pl.ds(first, width)], dst_ref=rights.at[where],
            send_sem=rsend.at[k], recv_sem=rrecv.at[k], device_id=peer(to))

    for k in range(1, PLANE):
        left_copy(k, lax.rem(q + k, PLANE), q).start()

    @pl.loop(1, members)
    def _(k):
        right_copy(k, lax.rem(slot + k, members), slot).start()

    left_own.wait()
    for k in range(1, PLANE):
        back = lax.rem(q + PLANE - k, PLANE)
        left_copy(k, back, back).wait_recv()

    def z_copy(way, n, a):
        to = blk + PLANE if way == 0 else blk - PLANE
        return pltpu.make_async_remote_copy(
            src_ref=staged.at[way, n, a], dst_ref=pool.at[PLANE + way * count + n, a],
            send_sem=zsend.at[way, n, a], recv_sem=zrecv.at[way, n, a],
            device_id={"blk": to, "grp": grp})

    ways = ((up_src, has_above, has_below), (down_src, has_below, has_above))
    for n in range(count):
        for a in range(width):
            for way, (source, sends, receives) in enumerate(ways):
                first = PLANE + way * count

                @pl.when(sends & receives)
                def _():
                    z_copy(way, n, a).wait_recv()

                @pl.when(sends)
                def _():
                    at = source[n]
                    value = pool[0, a]
                    for m in range(1, PLANE):
                        value = jnp.where(at == m, pool[m, a], value)
                    staged[way, n, a] = value

                    @pl.when(receives)
                    def _():
                        value = staged[way, n, a]
                        for m in range(n + 1):
                            value = jnp.where(at == first + m, pool[first + m, a], value)
                        staged[way, n, a] = value

                    z_copy(way, n, a).start()

    @pl.loop(1, members)
    def _(k):
        back = lax.rem(slot + members - k, members)
        right_copy(k, back, back).wait_recv()

    right_own.wait()
    for way, (source, sends, receives) in enumerate(ways):
        @pl.when(receives & jnp.logical_not(sends))
        def _():
            for n in range(count):
                for a in range(width):
                    z_copy(way, n, a).wait_recv()

    def part_copy(k, to):
        return pltpu.make_async_remote_copy(
            src_ref=parts.at[k], dst_ref=arrived.at[k], send_sem=psend.at[k],
            recv_sem=precv.at[k], device_id=peer(to))

    @pl.loop(1, members + 1)
    def _(k):
        t = lax.rem(slot + k, members)
        at = tile_at[t]
        psi = psis[t]
        total = jnp.zeros(psi.shape, jnp.float32)
        for a in range(width):
            inner = jnp.dot(pool[at, a], psi, preferred_element_type=jnp.float32)
            total += jnp.dot(inner.astype(jnp.bfloat16), rights[t, a], preferred_element_type=jnp.float32)
        parts[k] = total.astype(jnp.bfloat16)

        @pl.when(k < members)
        def _():
            part_copy(k, t).start()

    total = parts[members].astype(jnp.float32)
    for k in range(1, members):
        part_copy(k, lax.rem(slot + members - k, members)).wait_recv()
        total += arrived[k].astype(jnp.float32)
    live = live_mask_of(total.shape, own_size[0], own_size[1])
    out[0, 0] = jnp.where(live, total, 0.0).astype(jnp.bfloat16)

    for k in range(1, PLANE):
        left_copy(k, lax.rem(q + k, PLANE), q).wait_send()

    @pl.loop(1, members)
    def _(k):
        right_copy(k, lax.rem(slot + k, members), slot).wait_send()
        part_copy(k, lax.rem(slot + k, members)).wait_send()

    for way, (source, sends, receives) in enumerate(ways):
        @pl.when(sends)
        def _():
            for n in range(count):
                for a in range(width):
                    z_copy(way, n, a).wait_send()


SMEM = pl.BlockSpec(memory_space=pltpu.SMEM)
VMEM = pl.BlockSpec(memory_space=pltpu.VMEM)
ANY = pl.BlockSpec(memory_space=pl.ANY)
DMA = pltpu.SemaphoreType.DMA


def apply_call(count, planes, groups, up_src, down_src, tile_at, own_size, psis, left_env, right_env):
    side = psis.shape[-1]
    members = PLANE * groups
    width = left_env.shape[1] // PLANE
    return pl.pallas_call(
        functools.partial(apply_kernel, count, planes, groups),
        out_shape=jax.ShapeDtypeStruct((1, 1, side, side), jnp.bfloat16),
        in_specs=[SMEM] * 4 + [VMEM, ANY, ANY],
        out_specs=VMEM,
        scratch_shapes=[
            pltpu.VMEM((PLANE + 2 * count, width, side, side), jnp.bfloat16),
            pltpu.VMEM((2, count, width, side, side), jnp.bfloat16),
            pltpu.VMEM((members, width, side, side), jnp.bfloat16),
            pltpu.VMEM((members + 1, side, side), jnp.bfloat16),
            pltpu.VMEM((members, side, side), jnp.bfloat16),
            DMA((PLANE,)), DMA((PLANE,)), DMA((members,)), DMA((members,)),
            DMA((2, count, width)), DMA((2, count, width)), DMA((members,)), DMA((members,)),
            DMA((2,)),
        ],
        compiler_params=pltpu.CompilerParams(
            collective_id=count, has_side_effects=True, vmem_limit_bytes=48 * 1024 * 1024),
        name=f"apply_{count}",
    )(up_src, down_src, tile_at, own_size, psis, left_env, right_env)


def by_plane(left_env, right_env, psi, pairing, left_size, right_size):
    side = psi.shape[-1]
    groups = lax.axis_size("grp")
    blocks = lax.axis_size("blk")
    ranks, members, planes = blocks * groups, PLANE * groups, blocks // PLANE
    blk = lax.axis_index("blk")
    z = blk // PLANE
    table, psis = pl.pallas_call(
        functools.partial(spread_kernel, ranks, groups),
        out_shape=(
            jax.ShapeDtypeStruct((ranks, 8, 128), jnp.int32),
            jax.ShapeDtypeStruct((members, side, side), jnp.bfloat16),
        ),
        in_specs=[SMEM] * 3 + [VMEM],
        out_specs=(VMEM, VMEM),
        scratch_shapes=[
            pltpu.VMEM((8, 128), jnp.int32), pltpu.VMEM((ranks, 8, 128), jnp.int32),
            DMA((members,)), DMA((members,)), DMA((ranks,)), DMA((ranks,)),
        ],
        compiler_params=pltpu.CompilerParams(collective_id=0, has_side_effects=True),
        name="spread",
    )(pairing, left_size, right_size, psi)
    lefts = table[:, 0, 0]
    sectors = jnp.arange(blocks)
    home = sectors // PLANE
    level = jnp.arange(planes)
    same = lefts[:, None] == sectors[None, :]
    tile_plane = jnp.arange(ranks) // members
    far_up = jnp.max(jnp.where(same, tile_plane[:, None], -1), axis=0)
    far_down = jnp.min(jnp.where(same, tile_plane[:, None], planes), axis=0)
    need_up = (home[None] <= level[:, None]) & (far_up[None] > level[:, None])
    need_down = (home[None] >= level[:, None]) & (far_down[None] < level[:, None])
    key_up, key_down = (planes - far_up) * blocks + sectors, far_down * blocks + sectors
    place_up = jnp.sum(need_up[:, None, :] & (key_up[None, None, :] < key_up[None, :, None]), axis=2)
    place_down = jnp.sum(need_down[:, None, :] & (key_down[None, None, :] < key_down[None, :, None]), axis=2)
    most = jnp.maximum(jnp.max(jnp.sum(need_up, axis=1)), jnp.max(jnp.sum(need_down, axis=1)))
    own_size = jnp.stack([
        jnp.sum(jnp.where(sectors == pairing[0, 0], left_size, 0)), right_size[0]])

    def row(array, index):
        return jnp.sum(jnp.where(level[:, None] == index, array, 0), axis=0)

    from_below, from_above = row(place_up, z - 1), row(place_down, z + 1)
    own_lefts = jnp.sum(
        jnp.where(jnp.arange(ranks)[None] == z * members + jnp.arange(members)[:, None], lefts[None], 0), axis=1)
    out_up, out_down = row(place_up, z), row(place_down, z)
    has_up, has_down = row(need_up.astype(jnp.int32), z), row(need_down.astype(jnp.int32), z)

    def run(count, *tensors):
        where = jnp.where(
            home == z, sectors - z * PLANE,
            jnp.where(home < z, PLANE + from_below, PLANE + count + from_above))
        slots = jnp.arange(count)[:, None]
        up_src = jnp.sum(jnp.where((has_up[None] > 0) & (out_up[None] == slots), where[None], 0), axis=1)
        down_src = jnp.sum(jnp.where((has_down[None] > 0) & (out_down[None] == slots), where[None], 0), axis=1)
        tile_at = jnp.sum(jnp.where(own_lefts[:, None] == sectors[None], where[None], 0), axis=1)
        return apply_call(count, planes, groups, up_src, down_src, tile_at, own_size, *tensors)

    choice = jnp.sum(most > jnp.array(SLOTS[:-1]))
    return lax.switch(
        choice, [functools.partial(run, count) for count in SLOTS], psis, left_env, right_env)


def per_device(left_env, right_env, psi, pairing, left_size, right_size):
    tile_side = psi.shape[-1]
    per_right = psi.shape[1]
    groups = lax.axis_size("grp")
    channels = left_env.shape[1]
    left_count = left_size.shape[0]
    cells = jnp.arange(tile_side)
    own_lefts = pairing[0]
    matches = own_lefts[:, None] == jnp.arange(left_count)[None, :]
    own_rows = jnp.sum(jnp.where(matches, left_size[None, :], 0), axis=1)
    row_mask = cells[None, :] < own_rows[:, None]
    column_mask = cells < right_size[0]
    live_mask = row_mask[:, :, None] & column_mask[None, None, :]
    masked = jnp.where(live_mask, psi[0], jnp.zeros((), jnp.bfloat16))
    all_tiles, all_lefts = (
        lax.all_gather(masked, "grp", axis=0, tiled=True),
        lax.all_gather(own_lefts, "grp", axis=0, tiled=True),
    )
    pair_count = all_tiles.shape[0]
    by_left = jnp.argsort(all_lefts, stable=True)
    ranked = all_lefts[by_left]
    initial = jnp.zeros((pair_count, tile_side, channels, tile_side), jnp.bfloat16)
    incoming = lax.all_gather(left_env, "blk", axis=0, tiled=True)
    first_row = jnp.int32(0)
    row_count = incoming.shape[0]
    lower_end = jnp.sum(ranked < first_row)
    upper_end = jnp.sum(ranked < first_row + row_count)

    def absorb_one(position, gathered):
        pair_slot = by_left[position]
        sector_slot = ranked[position] - first_row
        left_block = lax.dynamic_index_in_dim(incoming, sector_slot, 0, keepdims=False)
        psi_tile = lax.dynamic_index_in_dim(all_tiles, pair_slot, 0, keepdims=False)
        contracted = jnp.einsum(
            "alk,kr->lar", left_block, psi_tile, preferred_element_type=jnp.float32
        ).astype(jnp.bfloat16)
        return lax.dynamic_update_index_in_dim(gathered, contracted, pair_slot, 0)

    contracted_all = lax.fori_loop(lower_end, upper_end, absorb_one, initial)
    sectioned = contracted_all.reshape(groups, per_right, tile_side, channels, tile_side)
    right_flat = right_env[0].reshape(-1, tile_side)
    received = lax.all_to_all(sectioned, "grp", split_axis=0, concat_axis=3, tiled=True)
    item_count = received.shape[1]
    flattened = received.reshape(item_count * tile_side, -1)
    product = jnp.dot(flattened, right_flat, preferred_element_type=jnp.float32).reshape(
        item_count, tile_side, tile_side
    )
    result = jnp.where(live_mask, product, jnp.zeros((), jnp.float32)).astype(jnp.bfloat16)
    return result[None]


def apply(left_env, *rest):
    blocks, groups = lax.axis_size("blk"), lax.axis_size("grp")
    planes = blocks // PLANE
    most = max(min(PLANE * (p + 1), PLANE * groups * (planes - 1 - p)) for p in range(planes))
    single = left_env.shape[0] == 1 and rest[1].shape[1] == 1
    fits = single and blocks % PLANE == 0 and left_env.shape[1] % PLANE == 0 and most <= SLOTS[-1]
    return (by_plane if fits else per_device)(left_env, *rest)


def solution(mesh):
    return jax.shard_map(
        apply,
        mesh=mesh,
        in_specs=(
            P("blk", "grp", None, None),
            P(("blk", "grp"), None, None, None),
            P(("blk", "grp"), None, None, None),
            P(("blk", "grp"), None),
            P(),
            P(("blk", "grp")),
        ),
        out_specs=P(("blk", "grp"), None, None, None),
        check_vma=False,
    )
```

```python
import functools

import jax
import jax.numpy as jnp
from jax import lax
from jax.experimental import pallas as pl
from jax.experimental.pallas import tpu as pltpu
from jax.sharding import PartitionSpec as P

PLANE = 4
SLOTS = (3, 4, 5, 8)


def live_mask_of(shape, rows, cols):
    row = lax.broadcasted_iota(jnp.int32, shape, 0)
    col = lax.broadcasted_iota(jnp.int32, shape, 1)
    return (row < rows) & (col < cols)


def spread_kernel(
    planes, groups, pairing, left_env, table_out, own_out,
    table, lsend, lrecv, psend, precv, zsend, zrecv, local,
):
    members = PLANE * groups
    width = own_out.shape[1]
    blk, grp = lax.axis_index("blk"), lax.axis_index("grp")
    z, q = blk // PLANE, lax.rem(blk, PLANE)
    slot = q * groups + grp

    def peer(index):
        return {"blk": z * PLANE + index // groups, "grp": lax.rem(index, groups)}

    def level(index):
        return {"blk": index * PLANE + q, "grp": grp}

    barrier = pltpu.get_barrier_semaphore()
    for k in range(1, members):
        pl.semaphore_signal(barrier, inc=1, device_id=peer(lax.rem(slot + k, members)))
    for k in range(1, planes):
        pl.semaphore_signal(barrier, inc=1, device_id=level(lax.rem(z + k, planes)))

    left_own = pltpu.make_async_copy(left_env.at[0, pl.ds(q * width, width)], own_out.at[q], local)
    left_own.start()
    table[z, slot] = jnp.full(table.shape[2:], pairing[0, 0], jnp.int32)
    pl.semaphore_wait(barrier, members + planes - 2)

    def entry(k, to, where):
        return pltpu.make_async_remote_copy(
            src_ref=table.at[z, where], dst_ref=table.at[z, where], send_sem=psend.at[k],
            recv_sem=precv.at[k], device_id=peer(to))

    def column(k, to, where):
        return pltpu.make_async_remote_copy(
            src_ref=table.at[where], dst_ref=table.at[where], send_sem=zsend.at[k],
            recv_sem=zrecv.at[k], device_id=level(to))

    def left_copy(k, to, where):
        return pltpu.make_async_remote_copy(
            src_ref=left_env.at[0, pl.ds(to * width, width)], dst_ref=own_out.at[where],
            send_sem=lsend.at[k], recv_sem=lrecv.at[k],
            device_id={"blk": z * PLANE + to, "grp": grp})

    for k in range(1, members):
        entry(k, lax.rem(slot + k, members), slot).start()
    for k in range(1, PLANE):
        left_copy(k, lax.rem(q + k, PLANE), q).start()
    for k in range(1, members):
        back = lax.rem(slot + members - k, members)
        entry(k, back, back).wait_recv()
    for k in range(1, planes):
        column(k, lax.rem(z + k, planes), z).start()
    for k in range(1, planes):
        back = lax.rem(z + planes - k, planes)
        column(k, back, back).wait_recv()
    table_out[...] = table[...]
    for k in range(1, members):
        entry(k, lax.rem(slot + k, members), slot).wait_send()
    for k in range(1, planes):
        column(k, lax.rem(z + k, planes), z).wait_send()
    left_own.wait()
    for k in range(1, PLANE):
        back = lax.rem(q + PLANE - k, PLANE)
        left_copy(k, back, back).wait_recv()
        left_copy(k, lax.rem(q + k, PLANE), q).wait_send()


def apply_kernel(
    count, planes, groups, up_src, down_src, tile_at, own_size, psi, own, right_env, out,
    pool, staged, rights, psis, parts, arrived,
    msend, mrecv, rsend, rrecv, zsend, zrecv, psend, precv, local,
):
    members = PLANE * groups
    width = pool.shape[1]
    blk, grp = lax.axis_index("blk"), lax.axis_index("grp")
    z, q = blk // PLANE, lax.rem(blk, PLANE)
    slot = q * groups + grp
    half = right_env.shape[1] // groups
    has_below, has_above = z > 0, z < planes - 1

    def peer(index):
        return {"blk": z * PLANE + index // groups, "grp": lax.rem(index, groups)}

    barrier = pltpu.get_barrier_semaphore()

    @pl.loop(1, members)
    def _(k):
        pl.semaphore_signal(barrier, inc=1, device_id=peer(lax.rem(slot + k, members)))

    @pl.when(has_below)
    def _():
        pl.semaphore_signal(barrier, inc=1, device_id={"blk": blk - PLANE, "grp": grp})

    @pl.when(has_above)
    def _():
        pl.semaphore_signal(barrier, inc=1, device_id={"blk": blk + PLANE, "grp": grp})

    left_own = pltpu.make_async_copy(own, pool.at[pl.ds(0, PLANE)], local.at[0])
    right_own = pltpu.make_async_copy(
        right_env.at[0, pl.ds(grp * half + q * width, width)], rights.at[slot], local.at[1])
    left_own.start()
    right_own.start()
    live = live_mask_of(psi.shape[2:], own_size[0], own_size[1])
    psis[slot] = jnp.where(live, psi[0, 0].astype(jnp.float32), 0.0).astype(jnp.bfloat16)
    pl.semaphore_wait(barrier, members - 1 + has_below.astype(jnp.int32) + has_above.astype(jnp.int32))

    def tile_copy(k, to, where):
        return pltpu.make_async_remote_copy(
            src_ref=psis.at[where], dst_ref=psis.at[where], send_sem=msend.at[k],
            recv_sem=mrecv.at[k], device_id=peer(to))

    def right_copy(k, to, where):
        first = lax.rem(to, groups) * half + to // groups * width
        return pltpu.make_async_remote_copy(
            src_ref=right_env.at[0, pl.ds(first, width)], dst_ref=rights.at[where],
            send_sem=rsend.at[k], recv_sem=rrecv.at[k], device_id=peer(to))

    def start_plane():
        @pl.loop(1, members)
        def _(k):
            tile_copy(k, lax.rem(slot + k, members), slot).start()
            right_copy(k, lax.rem(slot + k, members), slot).start()

    left_own.wait()

    def z_copy(way, n, a):
        to = blk + PLANE if way == 0 else blk - PLANE
        return pltpu.make_async_remote_copy(
            src_ref=staged.at[way, n, a], dst_ref=pool.at[PLANE + way * count + n, a],
            send_sem=zsend.at[way, n, a], recv_sem=zrecv.at[way, n, a],
            device_id={"blk": to, "grp": grp})

    def forward(way, n, a, source, receives):
        first = PLANE + way * count
        at = source[n]
        if receives:
            z_copy(way, n, a).wait_recv()
        value = pool[0, a]
        for m in range(1, PLANE):
            value = jnp.where(at == m, pool[m, a], value)
        if receives:
            for m in range(n + 1):
                value = jnp.where(at == first + m, pool[first + m, a], value)
        staged[way, n, a] = value
        z_copy(way, n, a).start()

    for level in range(planes):
        @pl.when(z == level)
        def _():
            steps = []
            for i in range(count * width):
                if level < planes - 1:
                    steps.append((i + level, level, 0, i))
                if level > 0:
                    steps.append((i + planes - 1 - level, planes - 1 - level, 1, i))
            started = False
            for _, hops, way, i in sorted(steps):
                if hops > 0 and not started:
                    start_plane()
                    started = True
                source = up_src if way == 0 else down_src
                forward(way, i // width, i % width, source, hops > 0)
            if not started:
                start_plane()

    @pl.loop(1, members)
    def _(k):
        back = lax.rem(slot + members - k, members)
        tile_copy(k, back, back).wait_recv()
        right_copy(k, back, back).wait_recv()

    right_own.wait()
    for way, ends in ((0, planes - 1), (1, 0)):
        @pl.when(z == ends)
        def _():
            for n in range(count):
                for a in range(width):
                    z_copy(way, n, a).wait_recv()

    def part_copy(k, to):
        return pltpu.make_async_remote_copy(
            src_ref=parts.at[k], dst_ref=arrived.at[k], send_sem=psend.at[k],
            recv_sem=precv.at[k], device_id=peer(to))

    @pl.loop(1, members + 1)
    def _(k):
        t = lax.rem(slot + k, members)
        at = tile_at[t]
        tile = psis[t]
        total = jnp.zeros(tile.shape, jnp.float32)
        for a in range(width):
            inner = jnp.dot(pool[at, a], tile, preferred_element_type=jnp.float32)
            total += jnp.dot(inner.astype(jnp.bfloat16), rights[t, a], preferred_element_type=jnp.float32)
        parts[k] = total.astype(jnp.bfloat16)

        @pl.when(k < members)
        def _():
            part_copy(k, t).start()

    total = parts[members].astype(jnp.float32)
    for k in range(1, members):
        part_copy(k, lax.rem(slot + members - k, members)).wait_recv()
        total += arrived[k].astype(jnp.float32)
    out[0, 0] = jnp.where(live, total, 0.0).astype(jnp.bfloat16)

    @pl.loop(1, members)
    def _(k):
        tile_copy(k, lax.rem(slot + k, members), slot).wait_send()
        right_copy(k, lax.rem(slot + k, members), slot).wait_send()
        part_copy(k, lax.rem(slot + k, members)).wait_send()

    for way, sends in ((0, has_above), (1, has_below)):
        @pl.when(sends)
        def _():
            for n in range(count):
                for a in range(width):
                    z_copy(way, n, a).wait_send()


SMEM = pl.BlockSpec(memory_space=pltpu.SMEM)
VMEM = pl.BlockSpec(memory_space=pltpu.VMEM)
ANY = pl.BlockSpec(memory_space=pl.ANY)
DMA = pltpu.SemaphoreType.DMA


def apply_call(count, planes, groups, up_src, down_src, tile_at, own_size, psi, own, right_env):
    side = psi.shape[-1]
    members = PLANE * groups
    width = own.shape[1]
    return pl.pallas_call(
        functools.partial(apply_kernel, count, planes, groups),
        out_shape=jax.ShapeDtypeStruct((1, 1, side, side), jnp.bfloat16),
        in_specs=[SMEM] * 4 + [VMEM, ANY, ANY],
        out_specs=VMEM,
        scratch_shapes=[
            pltpu.VMEM((PLANE + 2 * count, width, side, side), jnp.bfloat16),
            pltpu.VMEM((2, count, width, side, side), jnp.bfloat16),
            pltpu.VMEM((members, width, side, side), jnp.bfloat16),
            pltpu.VMEM((members, side, side), jnp.bfloat16),
            pltpu.VMEM((members + 1, side, side), jnp.bfloat16),
            pltpu.VMEM((members, side, side), jnp.bfloat16),
            DMA((members,)), DMA((members,)), DMA((members,)), DMA((members,)),
            DMA((2, count, width)), DMA((2, count, width)), DMA((members,)), DMA((members,)),
            DMA((2,)),
        ],
        compiler_params=pltpu.CompilerParams(
            collective_id=count, has_side_effects=True, vmem_limit_bytes=48 * 1024 * 1024),
        name=f"apply_{count}",
    )(up_src, down_src, tile_at, own_size, psi, own, right_env)


def by_plane(left_env, right_env, psi, pairing, left_size, right_size):
    side = psi.shape[-1]
    groups = lax.axis_size("grp")
    blocks = lax.axis_size("blk")
    ranks, members, planes = blocks * groups, PLANE * groups, blocks // PLANE
    blk = lax.axis_index("blk")
    z = blk // PLANE
    width = left_env.shape[1] // PLANE
    table, own = pl.pallas_call(
        functools.partial(spread_kernel, planes, groups),
        out_shape=(
            jax.ShapeDtypeStruct((planes, members, 8, 128), jnp.int32),
            jax.ShapeDtypeStruct((PLANE, width, side, side), jnp.bfloat16),
        ),
        in_specs=[SMEM, ANY],
        out_specs=(VMEM, ANY),
        scratch_shapes=[
            pltpu.VMEM((planes, members, 8, 128), jnp.int32),
            DMA((PLANE,)), DMA((PLANE,)), DMA((members,)), DMA((members,)),
            DMA((planes,)), DMA((planes,)), DMA(()),
        ],
        compiler_params=pltpu.CompilerParams(collective_id=0, has_side_effects=True),
        name="spread",
    )(pairing, left_env)
    lefts = table[:, :, 0, 0].reshape(-1)
    sectors = jnp.arange(blocks)
    home = sectors // PLANE
    level = jnp.arange(planes)
    same = lefts[:, None] == sectors[None, :]
    tile_plane = jnp.arange(ranks) // members
    far_up = jnp.max(jnp.where(same, tile_plane[:, None], -1), axis=0)
    far_down = jnp.min(jnp.where(same, tile_plane[:, None], planes), axis=0)
    need_up = (home[None] <= level[:, None]) & (far_up[None] > level[:, None])
    need_down = (home[None] >= level[:, None]) & (far_down[None] < level[:, None])
    key_up, key_down = (planes - far_up) * blocks + sectors, far_down * blocks + sectors
    place_up = jnp.sum(need_up[:, None, :] & (key_up[None, None, :] < key_up[None, :, None]), axis=2)
    place_down = jnp.sum(need_down[:, None, :] & (key_down[None, None, :] < key_down[None, :, None]), axis=2)
    most = jnp.maximum(jnp.max(jnp.sum(need_up, axis=1)), jnp.max(jnp.sum(need_down, axis=1)))
    own_size = jnp.stack([
        jnp.sum(jnp.where(sectors == pairing[0, 0], left_size, 0)), right_size[0]])

    def row(array, index):
        return jnp.sum(jnp.where(level[:, None] == index, array, 0), axis=0)

    from_below, from_above = row(place_up, z - 1), row(place_down, z + 1)
    own_lefts = jnp.sum(
        jnp.where(jnp.arange(ranks)[None] == z * members + jnp.arange(members)[:, None], lefts[None], 0), axis=1)
    out_up, out_down = row(place_up, z), row(place_down, z)
    has_up, has_down = row(need_up.astype(jnp.int32), z), row(need_down.astype(jnp.int32), z)

    def run(count, *tensors):
        where = jnp.where(
            home == z, sectors - z * PLANE,
            jnp.where(home < z, PLANE + from_below, PLANE + count + from_above))
        slots = jnp.arange(count)[:, None]
        up_src = jnp.sum(jnp.where((has_up[None] > 0) & (out_up[None] == slots), where[None], 0), axis=1)
        down_src = jnp.sum(jnp.where((has_down[None] > 0) & (out_down[None] == slots), where[None], 0), axis=1)
        tile_at = jnp.sum(jnp.where(own_lefts[:, None] == sectors[None], where[None], 0), axis=1)
        return apply_call(count, planes, groups, up_src, down_src, tile_at, own_size, *tensors)

    choice = jnp.sum(most > jnp.array(SLOTS[:-1]))
    return lax.switch(
        choice, [functools.partial(run, count) for count in SLOTS], psi, own, right_env)


def per_device(left_env, right_env, psi, pairing, left_size, right_size):
    tile_side = psi.shape[-1]
    per_right = psi.shape[1]
    groups = lax.axis_size("grp")
    channels = left_env.shape[1]
    left_count = left_size.shape[0]
    cells = jnp.arange(tile_side)
    own_lefts = pairing[0]
    matches = own_lefts[:, None] == jnp.arange(left_count)[None, :]
    own_rows = jnp.sum(jnp.where(matches, left_size[None, :], 0), axis=1)
    row_mask = cells[None, :] < own_rows[:, None]
    column_mask = cells < right_size[0]
    live_mask = row_mask[:, :, None] & column_mask[None, None, :]
    masked = jnp.where(live_mask, psi[0], jnp.zeros((), jnp.bfloat16))
    all_tiles, all_lefts = (
        lax.all_gather(masked, "grp", axis=0, tiled=True),
        lax.all_gather(own_lefts, "grp", axis=0, tiled=True),
    )
    pair_count = all_tiles.shape[0]
    by_left = jnp.argsort(all_lefts, stable=True)
    ranked = all_lefts[by_left]
    initial = jnp.zeros((pair_count, tile_side, channels, tile_side), jnp.bfloat16)
    incoming = lax.all_gather(left_env, "blk", axis=0, tiled=True)
    first_row = jnp.int32(0)
    row_count = incoming.shape[0]
    lower_end = jnp.sum(ranked < first_row)
    upper_end = jnp.sum(ranked < first_row + row_count)

    def absorb_one(position, gathered):
        pair_slot = by_left[position]
        sector_slot = ranked[position] - first_row
        left_block = lax.dynamic_index_in_dim(incoming, sector_slot, 0, keepdims=False)
        psi_tile = lax.dynamic_index_in_dim(all_tiles, pair_slot, 0, keepdims=False)
        contracted = jnp.einsum(
            "alk,kr->lar", left_block, psi_tile, preferred_element_type=jnp.float32
        ).astype(jnp.bfloat16)
        return lax.dynamic_update_index_in_dim(gathered, contracted, pair_slot, 0)

    contracted_all = lax.fori_loop(lower_end, upper_end, absorb_one, initial)
    sectioned = contracted_all.reshape(groups, per_right, tile_side, channels, tile_side)
    right_flat = right_env[0].reshape(-1, tile_side)
    received = lax.all_to_all(sectioned, "grp", split_axis=0, concat_axis=3, tiled=True)
    item_count = received.shape[1]
    flattened = received.reshape(item_count * tile_side, -1)
    product = jnp.dot(flattened, right_flat, preferred_element_type=jnp.float32).reshape(
        item_count, tile_side, tile_side
    )
    result = jnp.where(live_mask, product, jnp.zeros((), jnp.float32)).astype(jnp.bfloat16)
    return result[None]


def apply(left_env, *rest):
    blocks, groups = lax.axis_size("blk"), lax.axis_size("grp")
    planes = blocks // PLANE
    most = max(min(PLANE * (p + 1), PLANE * groups * (planes - 1 - p)) for p in range(planes))
    single = left_env.shape[0] == 1 and rest[1].shape[1] == 1
    fits = single and blocks % PLANE == 0 and left_env.shape[1] % PLANE == 0 and most <= SLOTS[-1]
    return (by_plane if fits else per_device)(left_env, *rest)


def solution(mesh):
    return jax.shard_map(
        apply,
        mesh=mesh,
        in_specs=(
            P("blk", "grp", None, None),
            P(("blk", "grp"), None, None, None),
            P(("blk", "grp"), None, None, None),
            P(("blk", "grp"), None),
            P(),
            P(("blk", "grp")),
        ),
        out_specs=P(("blk", "grp"), None, None, None),
        check_vma=False,
    )
```

```python
import functools

import jax
import jax.numpy as jnp
from jax import lax
from jax.experimental import pallas as pl
from jax.experimental.pallas import tpu as pltpu
from jax.sharding import PartitionSpec as P

PLANE = 4
SLOTS = (3, 4, 5, 8)


def live_mask_of(shape, rows, cols):
    row = lax.broadcasted_iota(jnp.int32, shape, 0)
    col = lax.broadcasted_iota(jnp.int32, shape, 1)
    return (row < rows) & (col < cols)


def spread_kernel(
    planes, groups, pairing, left_env, table_out, own_out,
    table, lsend, lrecv, psend, precv, zsend, zrecv, local,
):
    members = PLANE * groups
    width = own_out.shape[1]
    blk, grp = lax.axis_index("blk"), lax.axis_index("grp")
    z, q = blk // PLANE, lax.rem(blk, PLANE)
    slot = q * groups + grp

    def peer(index):
        return {"blk": z * PLANE + index // groups, "grp": lax.rem(index, groups)}

    def level(index):
        return {"blk": index * PLANE + q, "grp": grp}

    barrier = pltpu.get_barrier_semaphore()
    for k in range(1, members):
        pl.semaphore_signal(barrier, inc=1, device_id=peer(lax.rem(slot + k, members)))
    for k in range(1, planes):
        pl.semaphore_signal(barrier, inc=1, device_id=level(lax.rem(z + k, planes)))

    left_own = pltpu.make_async_copy(left_env.at[0, pl.ds(q * width, width)], own_out.at[q], local)
    left_own.start()
    table[z, slot] = jnp.full(table.shape[2:], pairing[0, 0], jnp.int32)
    pl.semaphore_wait(barrier, members + planes - 2)

    def entry(k, to, where):
        return pltpu.make_async_remote_copy(
            src_ref=table.at[z, where], dst_ref=table.at[z, where], send_sem=psend.at[k],
            recv_sem=precv.at[k], device_id=peer(to))

    def column(k, to, where):
        return pltpu.make_async_remote_copy(
            src_ref=table.at[where], dst_ref=table.at[where], send_sem=zsend.at[k],
            recv_sem=zrecv.at[k], device_id=level(to))

    def left_copy(k, to, where):
        return pltpu.make_async_remote_copy(
            src_ref=left_env.at[0, pl.ds(to * width, width)], dst_ref=own_out.at[where],
            send_sem=lsend.at[k], recv_sem=lrecv.at[k],
            device_id={"blk": z * PLANE + to, "grp": grp})

    for k in range(1, members):
        entry(k, lax.rem(slot + k, members), slot).start()
    for k in range(1, PLANE):
        left_copy(k, lax.rem(q + k, PLANE), q).start()
    for k in range(1, members):
        back = lax.rem(slot + members - k, members)
        entry(k, back, back).wait_recv()
    for k in range(1, planes):
        column(k, lax.rem(z + k, planes), z).start()
    for k in range(1, planes):
        back = lax.rem(z + planes - k, planes)
        column(k, back, back).wait_recv()
    table_out[...] = table[...]
    for k in range(1, members):
        entry(k, lax.rem(slot + k, members), slot).wait_send()
    for k in range(1, planes):
        column(k, lax.rem(z + k, planes), z).wait_send()
    left_own.wait()
    for k in range(1, PLANE):
        back = lax.rem(q + PLANE - k, PLANE)
        left_copy(k, back, back).wait_recv()
        left_copy(k, lax.rem(q + k, PLANE), q).wait_send()


def apply_kernel(
    count, planes, groups, up_src, down_src, tile_at, pairing, left_size, right_size, psi, own, right_env, out,
    pool, staged, rights, psis, given, taken, kept, joined, arrived,
    msend, mrecv, rsend, rrecv, zsend, zrecv, gsend, grecv, psend, precv, local,
):
    members = PLANE * groups
    width = pool.shape[1]
    blk, grp = lax.axis_index("blk"), lax.axis_index("grp")
    z, q = blk // PLANE, lax.rem(blk, PLANE)
    slot = q * groups + grp
    half = right_env.shape[1] // groups
    has_below, has_above = z > 0, z < planes - 1
    chips = members // 2
    core, chip = lax.rem(q, 2), q // 2 * groups + grp

    def member(on_chip, on_core):
        return (on_chip // groups * 2 + on_core) * groups + lax.rem(on_chip, groups)

    sibling = member(chip, 1 - core)

    def peer(index):
        return {"blk": z * PLANE + index // groups, "grp": lax.rem(index, groups)}

    barrier = pltpu.get_barrier_semaphore()

    @pl.loop(1, members)
    def _(k):
        pl.semaphore_signal(barrier, inc=1, device_id=peer(lax.rem(slot + k, members)))

    @pl.when(has_below)
    def _():
        pl.semaphore_signal(barrier, inc=1, device_id={"blk": blk - PLANE, "grp": grp})

    @pl.when(has_above)
    def _():
        pl.semaphore_signal(barrier, inc=1, device_id={"blk": blk + PLANE, "grp": grp})

    left_own = pltpu.make_async_copy(own, pool.at[pl.ds(0, PLANE)], local.at[0])
    right_own = pltpu.make_async_copy(
        right_env.at[0, pl.ds(grp * half + q * width, width)], rights.at[slot], local.at[1])
    left_own.start()
    right_own.start()
    live = live_mask_of(psi.shape[2:], left_size[pairing[0, 0]], right_size[0])
    psis[slot] = jnp.where(live, psi[0, 0].astype(jnp.float32), 0.0).astype(jnp.bfloat16)
    pl.semaphore_wait(barrier, members - 1 + has_below.astype(jnp.int32) + has_above.astype(jnp.int32))

    def tile_copy(k, to, where):
        return pltpu.make_async_remote_copy(
            src_ref=psis.at[where], dst_ref=psis.at[where], send_sem=msend.at[k],
            recv_sem=mrecv.at[k], device_id=peer(to))

    def right_copy(k, to, where):
        first = lax.rem(to, groups) * half + to // groups * width
        return pltpu.make_async_remote_copy(
            src_ref=right_env.at[0, pl.ds(first, width)], dst_ref=rights.at[where],
            send_sem=rsend.at[k], recv_sem=rrecv.at[k], device_id=peer(to))

    def start_plane():
        @pl.loop(1, chips)
        def _(d):
            tile_copy(d, member(lax.rem(chip + d, chips), core), slot).start()

        tile_copy(0, sibling, slot).start()

        @pl.loop(1, members)
        def _(k):
            right_copy(k, lax.rem(slot + k, members), slot).start()

    left_own.wait()

    def z_copy(way, n, a):
        to = blk + PLANE if way == 0 else blk - PLANE
        return pltpu.make_async_remote_copy(
            src_ref=staged.at[way, n, a], dst_ref=pool.at[PLANE + way * count + n, a],
            send_sem=zsend.at[way, n, a], recv_sem=zrecv.at[way, n, a],
            device_id={"blk": to, "grp": grp})

    def forward(way, n, a, source, receives):
        first = PLANE + way * count
        at = source[n]
        if receives:
            z_copy(way, n, a).wait_recv()
        value = pool[0, a]
        for m in range(1, PLANE):
            value = jnp.where(at == m, pool[m, a], value)
        if receives:
            for m in range(n + 1):
                value = jnp.where(at == first + m, pool[first + m, a], value)
        staged[way, n, a] = value
        z_copy(way, n, a).start()

    for level in range(planes):
        @pl.when(z == level)
        def _():
            steps = []
            for i in range(count * width):
                if level < planes - 1:
                    steps.append((i + level, level, 0, i))
                if level > 0:
                    steps.append((i + planes - 1 - level, planes - 1 - level, 1, i))
            started = False
            for _, hops, way, i in sorted(steps):
                if hops > 0 and not started:
                    start_plane()
                    started = True
                source = up_src if way == 0 else down_src
                forward(way, i // width, i % width, source, hops > 0)
            if not started:
                start_plane()

    @pl.loop(1, chips)
    def _(d):
        came = member(lax.rem(chip + chips - d, chips), core)
        tile_copy(d, came, came).wait_recv()
        tile_copy(chips + d, sibling, came).start()

    tile_copy(0, sibling, sibling).wait_recv()

    @pl.loop(1, chips)
    def _(d):
        came = member(lax.rem(chip + chips - d, chips), 1 - core)
        tile_copy(chips + d, sibling, came).wait_recv()

    right_own.wait()
    for way, ends in ((0, planes - 1), (1, 0)):
        @pl.when(z == ends)
        def _():
            for n in range(count):
                for a in range(width):
                    z_copy(way, n, a).wait_recv()

    def give_copy(d):
        return pltpu.make_async_remote_copy(
            src_ref=given.at[d], dst_ref=taken.at[d], send_sem=gsend.at[d],
            recv_sem=grecv.at[d], device_id=peer(sibling))

    def part_copy(d, to):
        return pltpu.make_async_remote_copy(
            src_ref=joined.at[d], dst_ref=arrived.at[d], send_sem=psend.at[d],
            recv_sem=precv.at[d], device_id=peer(to))

    def contract(t):
        at = tile_at[t]
        tile = psis[t]
        total = jnp.zeros(tile.shape, jnp.float32)
        for a in range(width):
            inner = jnp.dot(pool[at, a], tile, preferred_element_type=jnp.float32)
            total += jnp.dot(inner.astype(jnp.bfloat16), rights[t, a], preferred_element_type=jnp.float32)
        return total

    def wait_right(t):
        right_copy(lax.rem(slot + members - t, members), t, t).wait_recv()

    def join(d):
        give_copy(d).wait_recv()
        joined[d] = (kept[d] + taken[d].astype(jnp.float32)).astype(jnp.bfloat16)
        part_copy(d, member(lax.rem(chip + d, chips), core)).start()

    @pl.loop(1, chips + 1)
    def _(d):
        there = lax.rem(chip + d, chips)
        theirs, mine = member(there, 1 - core), member(there, core)
        wait_right(theirs)
        given[d] = contract(theirs).astype(jnp.bfloat16)
        give_copy(d).start()

        @pl.when(d < chips)
        def _():
            wait_right(mine)

        kept[d] = contract(mine)

        @pl.when(d > 1)
        def _():
            join(d - 1)

    give_copy(chips).wait_recv()
    total = kept[chips] + taken[chips].astype(jnp.float32)
    for d in range(1, chips):
        part_copy(d, member(lax.rem(chip + chips - d, chips), core)).wait_recv()
        total += arrived[d].astype(jnp.float32)
    out[0, 0] = jnp.where(live, total, 0.0).astype(jnp.bfloat16)

    @pl.loop(1, members)
    def _(k):
        right_copy(k, lax.rem(slot + k, members), slot).wait_send()

    tile_copy(0, sibling, slot).wait_send()

    @pl.loop(1, chips)
    def _(d):
        to = member(lax.rem(chip + d, chips), core)
        tile_copy(d, to, slot).wait_send()
        came = member(lax.rem(chip + chips - d, chips), core)
        tile_copy(chips + d, sibling, came).wait_send()
        part_copy(d, to).wait_send()

    @pl.loop(1, chips + 1)
    def _(d):
        give_copy(d).wait_send()

    for way, sends in ((0, has_above), (1, has_below)):
        @pl.when(sends)
        def _():
            for n in range(count):
                for a in range(width):
                    z_copy(way, n, a).wait_send()


SMEM = pl.BlockSpec(memory_space=pltpu.SMEM)
VMEM = pl.BlockSpec(memory_space=pltpu.VMEM)
ANY = pl.BlockSpec(memory_space=pl.ANY)
DMA = pltpu.SemaphoreType.DMA


def apply_call(count, planes, groups, up_src, down_src, tile_at, pairing, left_size, right_size, psi, own, right_env):
    side = psi.shape[-1]
    members = PLANE * groups
    width, chips = own.shape[1], members // 2
    return pl.pallas_call(
        functools.partial(apply_kernel, count, planes, groups),
        out_shape=jax.ShapeDtypeStruct((1, 1, side, side), jnp.bfloat16),
        in_specs=[SMEM] * 6 + [VMEM, ANY, ANY],
        out_specs=VMEM,
        scratch_shapes=[
            pltpu.VMEM((PLANE + 2 * count, width, side, side), jnp.bfloat16),
            pltpu.VMEM((2, count, width, side, side), jnp.bfloat16),
            pltpu.VMEM((members, width, side, side), jnp.bfloat16),
            pltpu.VMEM((members, side, side), jnp.bfloat16),
            pltpu.VMEM((chips + 1, side, side), jnp.bfloat16),
            pltpu.VMEM((chips + 1, side, side), jnp.bfloat16),
            pltpu.VMEM((chips + 1, side, side), jnp.float32),
            pltpu.VMEM((chips, side, side), jnp.bfloat16),
            pltpu.VMEM((chips, side, side), jnp.bfloat16),
            DMA((2 * chips,)), DMA((2 * chips,)), DMA((members,)), DMA((members,)),
            DMA((2, count, width)), DMA((2, count, width)), DMA((chips + 1,)), DMA((chips + 1,)),
            DMA((chips,)), DMA((chips,)),
            DMA((2,)),
        ],
        compiler_params=pltpu.CompilerParams(
            collective_id=count, has_side_effects=True, vmem_limit_bytes=48 * 1024 * 1024),
        name=f"apply_{count}",
    )(up_src, down_src, tile_at, pairing, left_size, right_size, psi, own, right_env)


def by_plane(left_env, right_env, psi, pairing, left_size, right_size):
    side = psi.shape[-1]
    groups = lax.axis_size("grp")
    blocks = lax.axis_size("blk")
    ranks, members, planes = blocks * groups, PLANE * groups, blocks // PLANE
    blk = lax.axis_index("blk")
    z = blk // PLANE
    width = left_env.shape[1] // PLANE
    table, own = pl.pallas_call(
        functools.partial(spread_kernel, planes, groups),
        out_shape=(
            jax.ShapeDtypeStruct((planes, members, 8, 128), jnp.int32),
            jax.ShapeDtypeStruct((PLANE, width, side, side), jnp.bfloat16),
        ),
        in_specs=[SMEM, ANY],
        out_specs=(VMEM, ANY),
        scratch_shapes=[
            pltpu.VMEM((planes, members, 8, 128), jnp.int32),
            DMA((PLANE,)), DMA((PLANE,)), DMA((members,)), DMA((members,)),
            DMA((planes,)), DMA((planes,)), DMA(()),
        ],
        compiler_params=pltpu.CompilerParams(collective_id=0, has_side_effects=True),
        name="spread",
    )(pairing, left_env)
    lefts = table[:, :, 0, 0].reshape(-1)
    sectors = jnp.arange(blocks)
    home = sectors // PLANE
    level = jnp.arange(planes)
    same = lefts[:, None] == sectors[None, :]
    tile_plane = jnp.arange(ranks) // members
    far_up = jnp.max(jnp.where(same, tile_plane[:, None], -1), axis=0)
    far_down = jnp.min(jnp.where(same, tile_plane[:, None], planes), axis=0)
    need_up = (home[None] <= level[:, None]) & (far_up[None] > level[:, None])
    need_down = (home[None] >= level[:, None]) & (far_down[None] < level[:, None])
    key_up, key_down = (planes - far_up) * blocks + sectors, far_down * blocks + sectors
    place_up = jnp.sum(need_up[:, None, :] & (key_up[None, None, :] < key_up[None, :, None]), axis=2)
    place_down = jnp.sum(need_down[:, None, :] & (key_down[None, None, :] < key_down[None, :, None]), axis=2)
    most = jnp.maximum(jnp.max(jnp.sum(need_up, axis=1)), jnp.max(jnp.sum(need_down, axis=1)))
    def row(array, index):
        return jnp.sum(jnp.where(level[:, None] == index, array, 0), axis=0)

    from_below, from_above = row(place_up, z - 1), row(place_down, z + 1)
    own_lefts = jnp.sum(
        jnp.where(jnp.arange(ranks)[None] == z * members + jnp.arange(members)[:, None], lefts[None], 0), axis=1)
    out_up, out_down = row(place_up, z), row(place_down, z)
    has_up, has_down = row(need_up.astype(jnp.int32), z), row(need_down.astype(jnp.int32), z)

    def run(count, *operands):
        where = jnp.where(
            home == z, sectors - z * PLANE,
            jnp.where(home < z, PLANE + from_below, PLANE + count + from_above))
        slots = jnp.arange(count)[:, None]
        up_src = jnp.sum(jnp.where((has_up[None] > 0) & (out_up[None] == slots), where[None], 0), axis=1)
        down_src = jnp.sum(jnp.where((has_down[None] > 0) & (out_down[None] == slots), where[None], 0), axis=1)
        tile_at = jnp.sum(jnp.where(own_lefts[:, None] == sectors[None], where[None], 0), axis=1)
        return apply_call(count, planes, groups, up_src, down_src, tile_at, *operands)

    choice = jnp.sum(most > jnp.array(SLOTS[:-1]))
    return lax.switch(
        choice, [functools.partial(run, count) for count in SLOTS],
        pairing, left_size, right_size, psi, own, right_env)


def per_device(left_env, right_env, psi, pairing, left_size, right_size):
    tile_side = psi.shape[-1]
    per_right = psi.shape[1]
    groups = lax.axis_size("grp")
    channels = left_env.shape[1]
    left_count = left_size.shape[0]
    cells = jnp.arange(tile_side)
    own_lefts = pairing[0]
    matches = own_lefts[:, None] == jnp.arange(left_count)[None, :]
    own_rows = jnp.sum(jnp.where(matches, left_size[None, :], 0), axis=1)
    row_mask = cells[None, :] < own_rows[:, None]
    column_mask = cells < right_size[0]
    live_mask = row_mask[:, :, None] & column_mask[None, None, :]
    masked = jnp.where(live_mask, psi[0], jnp.zeros((), jnp.bfloat16))
    all_tiles, all_lefts = (
        lax.all_gather(masked, "grp", axis=0, tiled=True),
        lax.all_gather(own_lefts, "grp", axis=0, tiled=True),
    )
    pair_count = all_tiles.shape[0]
    by_left = jnp.argsort(all_lefts, stable=True)
    ranked = all_lefts[by_left]
    initial = jnp.zeros((pair_count, tile_side, channels, tile_side), jnp.bfloat16)
    incoming = lax.all_gather(left_env, "blk", axis=0, tiled=True)
    first_row = jnp.int32(0)
    row_count = incoming.shape[0]
    lower_end = jnp.sum(ranked < first_row)
    upper_end = jnp.sum(ranked < first_row + row_count)

    def absorb_one(position, gathered):
        pair_slot = by_left[position]
        sector_slot = ranked[position] - first_row
        left_block = lax.dynamic_index_in_dim(incoming, sector_slot, 0, keepdims=False)
        psi_tile = lax.dynamic_index_in_dim(all_tiles, pair_slot, 0, keepdims=False)
        contracted = jnp.einsum(
            "alk,kr->lar", left_block, psi_tile, preferred_element_type=jnp.float32
        ).astype(jnp.bfloat16)
        return lax.dynamic_update_index_in_dim(gathered, contracted, pair_slot, 0)

    contracted_all = lax.fori_loop(lower_end, upper_end, absorb_one, initial)
    sectioned = contracted_all.reshape(groups, per_right, tile_side, channels, tile_side)
    right_flat = right_env[0].reshape(-1, tile_side)
    received = lax.all_to_all(sectioned, "grp", split_axis=0, concat_axis=3, tiled=True)
    item_count = received.shape[1]
    flattened = received.reshape(item_count * tile_side, -1)
    product = jnp.dot(flattened, right_flat, preferred_element_type=jnp.float32).reshape(
        item_count, tile_side, tile_side
    )
    result = jnp.where(live_mask, product, jnp.zeros((), jnp.float32)).astype(jnp.bfloat16)
    return result[None]


def apply(left_env, *rest):
    blocks, groups = lax.axis_size("blk"), lax.axis_size("grp")
    planes = blocks // PLANE
    most = max(min(PLANE * (p + 1), PLANE * groups * (planes - 1 - p)) for p in range(planes))
    single = left_env.shape[0] == 1 and rest[1].shape[1] == 1
    fits = single and blocks % PLANE == 0 and left_env.shape[1] % PLANE == 0 and most <= SLOTS[-1]
    return (by_plane if fits else per_device)(left_env, *rest)


def solution(mesh):
    return jax.shard_map(
        apply,
        mesh=mesh,
        in_specs=(
            P("blk", "grp", None, None),
            P(("blk", "grp"), None, None, None),
            P(("blk", "grp"), None, None, None),
            P(("blk", "grp"), None),
            P(),
            P(("blk", "grp")),
        ),
        out_specs=P(("blk", "grp"), None, None, None),
        check_vma=False,
    )
```

```python
import functools

import jax
import jax.numpy as jnp
from jax import lax
from jax.experimental import pallas as pl
from jax.experimental.pallas import tpu as pltpu
from jax.sharding import PartitionSpec as P

PLANE = 4
ABOVE = 64
SLOTS = (3, 4, 5, 8)


def live_mask_of(shape, rows, cols):
    row = lax.broadcasted_iota(jnp.int32, shape, 0)
    col = lax.broadcasted_iota(jnp.int32, shape, 1)
    return (row < rows) & (col < cols)


def plan_of(planes, groups, z, table):
    members, blocks = PLANE * groups, planes * PLANE
    shape = (blocks, 128)
    sub = lax.broadcasted_iota(jnp.int32, shape, 0)
    lane = lax.broadcasted_iota(jnp.int32, shape, 1)

    def spread(value):
        return jnp.broadcast_to(value[:1], shape)

    def facts(sector):
        up, down = jnp.full(shape, -1, jnp.int32), jnp.full(shape, planes, jnp.int32)
        for p in range(planes):
            here = jnp.zeros(shape, jnp.int32)
            for t in range(members):
                here = jnp.where(spread(table[p, t]) == sector, 1, here)
            up = jnp.where(here > 0, p, up)
            down = jnp.where((here > 0) & (down == planes), p, down)
        home = sector // PLANE
        return home, up, down, (planes - up) * blocks + sector, down * blocks + sector

    home_s, up_s, down_s, key_up_s, key_down_s = facts(sub)
    home_l, up_l, down_l, key_up_l, key_down_l = facts(lane)

    def need(home, far, p, upward):
        return (home <= p) & (far > p) if upward else (home >= p) & (far < p)

    def place(p, upward):
        keys, mine = (key_up_l, key_up_s) if upward else (key_down_l, key_down_s)
        before = need(home_l, up_l if upward else down_l, p, upward) & (keys < mine)
        count = jnp.sum(jnp.where(before, 1.0, 0.0), axis=1, keepdims=True)
        return jnp.broadcast_to(count, shape).astype(jnp.int32)

    where = jnp.where(
        home_s == z, sub - z * PLANE,
        jnp.where(home_s < z, PLANE + place(z - 1, True), ABOVE + place(z + 1, False)))

    def total(values):
        return jnp.sum(values.astype(jnp.float32), axis=0, keepdims=True).astype(jnp.int32)

    def sources(upward):
        out = need(home_s, up_s if upward else down_s, z, upward) & (place(z, upward) == lane)
        return total(jnp.where(out, where, 0))

    lefts = jnp.full(shape, -1, jnp.int32)
    for t in range(members):
        lefts = jnp.where(lane == t, spread(table[z, t]), lefts)
    most = jnp.zeros((1, 128), jnp.int32)
    for p in range(planes):
        most = jnp.maximum(most, total(jnp.where(need(home_s, up_s, p, True), 1, 0)))
        most = jnp.maximum(most, total(jnp.where(need(home_s, down_s, p, False), 1, 0)))
    rows = (sources(True), sources(False), total(jnp.where(lefts == sub, where, 0)), most)
    out = jnp.zeros((8, 128), jnp.int32)
    row = lax.broadcasted_iota(jnp.int32, out.shape, 0)
    for index, value in enumerate(rows):
        out = jnp.where(row == index, jnp.broadcast_to(value, out.shape), out)
    return out


def spread_kernel(
    planes, groups, pairing, left_env, plan_out, own_out,
    table, lsend, lrecv, psend, precv, zsend, zrecv, local,
):
    members = PLANE * groups
    width = own_out.shape[1]
    blk, grp = lax.axis_index("blk"), lax.axis_index("grp")
    z, q = blk // PLANE, lax.rem(blk, PLANE)
    slot = q * groups + grp

    def peer(index):
        return {"blk": z * PLANE + index // groups, "grp": lax.rem(index, groups)}

    def level(index):
        return {"blk": index * PLANE + q, "grp": grp}

    barrier = pltpu.get_barrier_semaphore()
    for k in range(1, members):
        pl.semaphore_signal(barrier, inc=1, device_id=peer(lax.rem(slot + k, members)))
    for k in range(1, planes):
        pl.semaphore_signal(barrier, inc=1, device_id=level(lax.rem(z + k, planes)))

    left_own = pltpu.make_async_copy(left_env.at[0, pl.ds(q * width, width)], own_out.at[q], local)
    left_own.start()
    table[z, slot] = jnp.full(table.shape[2:], pairing[0, 0], jnp.int32)
    pl.semaphore_wait(barrier, members + planes - 2)

    def entry(k, to, where):
        return pltpu.make_async_remote_copy(
            src_ref=table.at[z, where], dst_ref=table.at[z, where], send_sem=psend.at[k],
            recv_sem=precv.at[k], device_id=peer(to))

    def column(k, to, where):
        return pltpu.make_async_remote_copy(
            src_ref=table.at[where], dst_ref=table.at[where], send_sem=zsend.at[k],
            recv_sem=zrecv.at[k], device_id=level(to))

    def left_copy(k, to, where):
        return pltpu.make_async_remote_copy(
            src_ref=left_env.at[0, pl.ds(to * width, width)], dst_ref=own_out.at[where],
            send_sem=lsend.at[k], recv_sem=lrecv.at[k],
            device_id={"blk": z * PLANE + to, "grp": grp})

    for k in range(1, members):
        entry(k, lax.rem(slot + k, members), slot).start()
    for k in range(1, PLANE):
        left_copy(k, lax.rem(q + k, PLANE), q).start()
    for k in range(1, members):
        back = lax.rem(slot + members - k, members)
        entry(k, back, back).wait_recv()
    for k in range(1, planes):
        column(k, lax.rem(z + k, planes), z).start()
    for k in range(1, planes):
        back = lax.rem(z + planes - k, planes)
        column(k, back, back).wait_recv()
    plan_out[...] = plan_of(planes, groups, z, table)
    for k in range(1, members):
        entry(k, lax.rem(slot + k, members), slot).wait_send()
    for k in range(1, planes):
        column(k, lax.rem(z + k, planes), z).wait_send()
    left_own.wait()
    for k in range(1, PLANE):
        back = lax.rem(q + PLANE - k, PLANE)
        left_copy(k, back, back).wait_recv()
        left_copy(k, lax.rem(q + k, PLANE), q).wait_send()


def apply_kernel(
    count, planes, groups, plan, pairing, left_size, right_size, psi, own, right_env, out,
    pool, staged, rights, psis, given, taken, kept, joined, arrived,
    msend, mrecv, rsend, rrecv, zsend, zrecv, gsend, grecv, psend, precv, local,
):
    members = PLANE * groups
    width = pool.shape[1]
    blk, grp = lax.axis_index("blk"), lax.axis_index("grp")
    z, q = blk // PLANE, lax.rem(blk, PLANE)
    slot = q * groups + grp
    half = right_env.shape[1] // groups
    has_below, has_above = z > 0, z < planes - 1
    chips = members // 2
    core, chip = lax.rem(q, 2), q // 2 * groups + grp

    def member(on_chip, on_core):
        return (on_chip // groups * 2 + on_core) * groups + lax.rem(on_chip, groups)

    sibling = member(chip, 1 - core)

    def peer(index):
        return {"blk": z * PLANE + index // groups, "grp": lax.rem(index, groups)}

    barrier = pltpu.get_barrier_semaphore()

    @pl.loop(1, members)
    def _(k):
        pl.semaphore_signal(barrier, inc=1, device_id=peer(lax.rem(slot + k, members)))

    @pl.when(has_below)
    def _():
        pl.semaphore_signal(barrier, inc=1, device_id={"blk": blk - PLANE, "grp": grp})

    @pl.when(has_above)
    def _():
        pl.semaphore_signal(barrier, inc=1, device_id={"blk": blk + PLANE, "grp": grp})

    left_own = pltpu.make_async_copy(own, pool.at[pl.ds(0, PLANE)], local.at[0])
    right_own = pltpu.make_async_copy(
        right_env.at[0, pl.ds(grp * half + q * width, width)], rights.at[slot], local.at[1])
    left_own.start()
    right_own.start()
    live = live_mask_of(psi.shape[2:], left_size[pairing[0, 0]], right_size[0])
    psis[slot] = jnp.where(live, psi[0, 0].astype(jnp.float32), 0.0).astype(jnp.bfloat16)
    pl.semaphore_wait(barrier, members - 1 + has_below.astype(jnp.int32) + has_above.astype(jnp.int32))

    def tile_copy(k, to, where):
        return pltpu.make_async_remote_copy(
            src_ref=psis.at[where], dst_ref=psis.at[where], send_sem=msend.at[k],
            recv_sem=mrecv.at[k], device_id=peer(to))

    def right_copy(k, to, where):
        first = lax.rem(to, groups) * half + to // groups * width
        return pltpu.make_async_remote_copy(
            src_ref=right_env.at[0, pl.ds(first, width)], dst_ref=rights.at[where],
            send_sem=rsend.at[k], recv_sem=rrecv.at[k], device_id=peer(to))

    def start_plane():
        @pl.loop(1, chips)
        def _(d):
            tile_copy(d, member(lax.rem(chip + d, chips), core), slot).start()

        tile_copy(0, sibling, slot).start()

        @pl.loop(1, members)
        def _(k):
            right_copy(k, lax.rem(slot + k, members), slot).start()

    left_own.wait()

    def z_copy(way, n, a):
        to = blk + PLANE if way == 0 else blk - PLANE
        return pltpu.make_async_remote_copy(
            src_ref=staged.at[way, n, a], dst_ref=pool.at[PLANE + way * count + n, a],
            send_sem=zsend.at[way, n, a], recv_sem=zrecv.at[way, n, a],
            device_id={"blk": to, "grp": grp})

    def placed(at):
        return jnp.where(at >= ABOVE, at - ABOVE + PLANE + count, at)

    def forward(way, n, a, receives):
        first = PLANE + way * count
        at = placed(plan[way, n])
        if receives:
            z_copy(way, n, a).wait_recv()
        value = pool[0, a]
        for m in range(1, PLANE):
            value = jnp.where(at == m, pool[m, a], value)
        if receives:
            for m in range(n + 1):
                value = jnp.where(at == first + m, pool[first + m, a], value)
        staged[way, n, a] = value
        z_copy(way, n, a).start()

    for level in range(planes):
        @pl.when(z == level)
        def _():
            steps = []
            for i in range(count * width):
                if level < planes - 1:
                    steps.append((i + level, level, 0, i))
                if level > 0:
                    steps.append((i + planes - 1 - level, planes - 1 - level, 1, i))
            started = False
            for _, hops, way, i in sorted(steps):
                if hops > 0 and not started:
                    start_plane()
                    started = True
                forward(way, i // width, i % width, hops > 0)
            if not started:
                start_plane()

    @pl.loop(1, chips)
    def _(d):
        came = member(lax.rem(chip + chips - d, chips), core)
        tile_copy(d, came, came).wait_recv()
        tile_copy(chips + d, sibling, came).start()

    tile_copy(0, sibling, sibling).wait_recv()

    @pl.loop(1, chips)
    def _(d):
        came = member(lax.rem(chip + chips - d, chips), 1 - core)
        tile_copy(chips + d, sibling, came).wait_recv()

    right_own.wait()
    for way, ends in ((0, planes - 1), (1, 0)):
        @pl.when(z == ends)
        def _():
            for n in range(count):
                for a in range(width):
                    z_copy(way, n, a).wait_recv()

    def give_copy(d):
        return pltpu.make_async_remote_copy(
            src_ref=given.at[d], dst_ref=taken.at[d], send_sem=gsend.at[d],
            recv_sem=grecv.at[d], device_id=peer(sibling))

    def part_copy(d, to):
        return pltpu.make_async_remote_copy(
            src_ref=joined.at[d], dst_ref=arrived.at[d], send_sem=psend.at[d],
            recv_sem=precv.at[d], device_id=peer(to))

    def contract(t):
        at = placed(plan[2, t])
        tile = psis[t]
        total = jnp.zeros(tile.shape, jnp.float32)
        for a in range(width):
            inner = jnp.dot(pool[at, a], tile, preferred_element_type=jnp.float32)
            total += jnp.dot(inner.astype(jnp.bfloat16), rights[t, a], preferred_element_type=jnp.float32)
        return total

    def wait_right(t):
        right_copy(lax.rem(slot + members - t, members), t, t).wait_recv()

    def join(d):
        give_copy(d).wait_recv()
        joined[d] = (kept[d] + taken[d].astype(jnp.float32)).astype(jnp.bfloat16)
        part_copy(d, member(lax.rem(chip + d, chips), core)).start()

    @pl.loop(1, chips + 1)
    def _(d):
        there = lax.rem(chip + d, chips)
        theirs, mine = member(there, 1 - core), member(there, core)
        wait_right(theirs)
        given[d] = contract(theirs).astype(jnp.bfloat16)
        give_copy(d).start()

        @pl.when(d < chips)
        def _():
            wait_right(mine)

        kept[d] = contract(mine)

        @pl.when(d > 1)
        def _():
            join(d - 1)

    give_copy(chips).wait_recv()
    total = kept[chips] + taken[chips].astype(jnp.float32)
    for d in range(1, chips):
        part_copy(d, member(lax.rem(chip + chips - d, chips), core)).wait_recv()
        total += arrived[d].astype(jnp.float32)
    out[0, 0] = jnp.where(live, total, 0.0).astype(jnp.bfloat16)

    @pl.loop(1, members)
    def _(k):
        right_copy(k, lax.rem(slot + k, members), slot).wait_send()

    tile_copy(0, sibling, slot).wait_send()

    @pl.loop(1, chips)
    def _(d):
        to = member(lax.rem(chip + d, chips), core)
        tile_copy(d, to, slot).wait_send()
        came = member(lax.rem(chip + chips - d, chips), core)
        tile_copy(chips + d, sibling, came).wait_send()
        part_copy(d, to).wait_send()

    @pl.loop(1, chips + 1)
    def _(d):
        give_copy(d).wait_send()

    for way, sends in ((0, has_above), (1, has_below)):
        @pl.when(sends)
        def _():
            for n in range(count):
                for a in range(width):
                    z_copy(way, n, a).wait_send()


SMEM = pl.BlockSpec(memory_space=pltpu.SMEM)
VMEM = pl.BlockSpec(memory_space=pltpu.VMEM)
ANY = pl.BlockSpec(memory_space=pl.ANY)
DMA = pltpu.SemaphoreType.DMA


def apply_call(count, planes, groups, plan, pairing, left_size, right_size, psi, own, right_env):
    side = psi.shape[-1]
    members = PLANE * groups
    width, chips = own.shape[1], members // 2
    return pl.pallas_call(
        functools.partial(apply_kernel, count, planes, groups),
        out_shape=jax.ShapeDtypeStruct((1, 1, side, side), jnp.bfloat16),
        in_specs=[SMEM] * 4 + [VMEM, ANY, ANY],
        out_specs=VMEM,
        scratch_shapes=[
            pltpu.VMEM((PLANE + 2 * count, width, side, side), jnp.bfloat16),
            pltpu.VMEM((2, count, width, side, side), jnp.bfloat16),
            pltpu.VMEM((members, width, side, side), jnp.bfloat16),
            pltpu.VMEM((members, side, side), jnp.bfloat16),
            pltpu.VMEM((chips + 1, side, side), jnp.bfloat16),
            pltpu.VMEM((chips + 1, side, side), jnp.bfloat16),
            pltpu.VMEM((chips + 1, side, side), jnp.float32),
            pltpu.VMEM((chips, side, side), jnp.bfloat16),
            pltpu.VMEM((chips, side, side), jnp.bfloat16),
            DMA((2 * chips,)), DMA((2 * chips,)), DMA((members,)), DMA((members,)),
            DMA((2, count, width)), DMA((2, count, width)), DMA((chips + 1,)), DMA((chips + 1,)),
            DMA((chips,)), DMA((chips,)),
            DMA((2,)),
        ],
        compiler_params=pltpu.CompilerParams(
            collective_id=count, has_side_effects=True, vmem_limit_bytes=48 * 1024 * 1024),
        name=f"apply_{count}",
    )(plan, pairing, left_size, right_size, psi, own, right_env)


def by_plane(left_env, right_env, psi, pairing, left_size, right_size):
    side = psi.shape[-1]
    groups = lax.axis_size("grp")
    blocks = lax.axis_size("blk")
    members, planes = PLANE * groups, blocks // PLANE
    width = left_env.shape[1] // PLANE
    plan, own = pl.pallas_call(
        functools.partial(spread_kernel, planes, groups),
        out_shape=(
            jax.ShapeDtypeStruct((8, 128), jnp.int32),
            jax.ShapeDtypeStruct((PLANE, width, side, side), jnp.bfloat16),
        ),
        in_specs=[SMEM, ANY],
        out_specs=(VMEM, ANY),
        scratch_shapes=[
            pltpu.VMEM((planes, members, 8, 128), jnp.int32),
            DMA((PLANE,)), DMA((PLANE,)), DMA((members,)), DMA((members,)),
            DMA((planes,)), DMA((planes,)), DMA(()),
        ],
        compiler_params=pltpu.CompilerParams(collective_id=0, has_side_effects=True),
        name="spread",
    )(pairing, left_env)
    choice = jnp.int32(0)
    for count in SLOTS[:-1]:
        choice += (plan[3, 0] > count).astype(jnp.int32)
    return lax.switch(
        choice, [functools.partial(apply_call, count, planes, groups) for count in SLOTS],
        plan, pairing, left_size, right_size, psi, own, right_env)


def per_device(left_env, right_env, psi, pairing, left_size, right_size):
    tile_side = psi.shape[-1]
    per_right = psi.shape[1]
    groups = lax.axis_size("grp")
    channels = left_env.shape[1]
    left_count = left_size.shape[0]
    cells = jnp.arange(tile_side)
    own_lefts = pairing[0]
    matches = own_lefts[:, None] == jnp.arange(left_count)[None, :]
    own_rows = jnp.sum(jnp.where(matches, left_size[None, :], 0), axis=1)
    row_mask = cells[None, :] < own_rows[:, None]
    column_mask = cells < right_size[0]
    live_mask = row_mask[:, :, None] & column_mask[None, None, :]
    masked = jnp.where(live_mask, psi[0], jnp.zeros((), jnp.bfloat16))
    all_tiles, all_lefts = (
        lax.all_gather(masked, "grp", axis=0, tiled=True),
        lax.all_gather(own_lefts, "grp", axis=0, tiled=True),
    )
    pair_count = all_tiles.shape[0]
    by_left = jnp.argsort(all_lefts, stable=True)
    ranked = all_lefts[by_left]
    initial = jnp.zeros((pair_count, tile_side, channels, tile_side), jnp.bfloat16)
    incoming = lax.all_gather(left_env, "blk", axis=0, tiled=True)
    first_row = jnp.int32(0)
    row_count = incoming.shape[0]
    lower_end = jnp.sum(ranked < first_row)
    upper_end = jnp.sum(ranked < first_row + row_count)

    def absorb_one(position, gathered):
        pair_slot = by_left[position]
        sector_slot = ranked[position] - first_row
        left_block = lax.dynamic_index_in_dim(incoming, sector_slot, 0, keepdims=False)
        psi_tile = lax.dynamic_index_in_dim(all_tiles, pair_slot, 0, keepdims=False)
        contracted = jnp.einsum(
            "alk,kr->lar", left_block, psi_tile, preferred_element_type=jnp.float32
        ).astype(jnp.bfloat16)
        return lax.dynamic_update_index_in_dim(gathered, contracted, pair_slot, 0)

    contracted_all = lax.fori_loop(lower_end, upper_end, absorb_one, initial)
    sectioned = contracted_all.reshape(groups, per_right, tile_side, channels, tile_side)
    right_flat = right_env[0].reshape(-1, tile_side)
    received = lax.all_to_all(sectioned, "grp", split_axis=0, concat_axis=3, tiled=True)
    item_count = received.shape[1]
    flattened = received.reshape(item_count * tile_side, -1)
    product = jnp.dot(flattened, right_flat, preferred_element_type=jnp.float32).reshape(
        item_count, tile_side, tile_side
    )
    result = jnp.where(live_mask, product, jnp.zeros((), jnp.float32)).astype(jnp.bfloat16)
    return result[None]


def apply(left_env, *rest):
    blocks, groups = lax.axis_size("blk"), lax.axis_size("grp")
    planes = blocks // PLANE
    most = max(min(PLANE * (p + 1), PLANE * groups * (planes - 1 - p)) for p in range(planes))
    single = left_env.shape[0] == 1 and rest[1].shape[1] == 1
    fits = single and blocks % PLANE == 0 and left_env.shape[1] % PLANE == 0 and most <= SLOTS[-1]
    return (by_plane if fits else per_device)(left_env, *rest)


def solution(mesh):
    return jax.shard_map(
        apply,
        mesh=mesh,
        in_specs=(
            P("blk", "grp", None, None),
            P(("blk", "grp"), None, None, None),
            P(("blk", "grp"), None, None, None),
            P(("blk", "grp"), None),
            P(),
            P(("blk", "grp")),
        ),
        out_specs=P(("blk", "grp"), None, None, None),
        check_vma=False,
    )
```
